256 devices in a mesh: seq: 64 (over z, x, y_lo), ch: 4 (over y_hi, core).
Axes of the slice: x: 4, y: 4 (y_hi: 2, y_lo: 2; y = y_hi * 2 + y_lo), z: 8, core: 2. Of those that a mesh axis runs over, the one named last changes fastest.
Arguments:
- stream: bfloat16 [1, 768, 262144], P(None, 'ch', 'seq'), may hold values from -40 to 40
- in_weight: float32 [768], P('ch'), may hold values from -4 to 4
- in_bias: float32 [768], P('ch'), may hold values from -2 to 2
- out_weight: float32 [768], P('ch'), may hold values from -4 to 4
- out_bias: float32 [768], P('ch'), may hold values from -2 to 2
- first_mix: bfloat16 [512, 512], replicated, may hold values from -0.25 to 0.25
- twist_in: bfloat16 [512, 512], P(None, 'seq'), may hold values from -4 to 4
- second_mix: bfloat16 [512, 512], replicated, may hold values from -0.25 to 0.25
- kernel: bfloat16 [768, 512, 512], P('ch', 'seq'), may hold values from -4 to 4
- third_mix: bfloat16 [512, 512], replicated, may hold values from -0.25 to 0.25
- twist_out: bfloat16 [512, 512], P(None, 'seq'), may hold values from -4 to 4
- fourth_mix: bfloat16 [512, 512], replicated, may hold values from -0.25 to 0.25
- norm_gain: bfloat16 [768], replicated, may hold values from 0.5 to 2
- gate_weight: bfloat16 [4, 192, 768], replicated, may hold values from -0.4375 to 0.4375
- up_weight: bfloat16 [4, 192, 768], replicated, may hold values from -0.4375 to 0.4375
- down_weight: bfloat16 [4, 192, 768], replicated, may hold values from -0.21875 to 0.21875
Outputs:
- layer_out: bfloat16 [1, 768, 262144], P(None, 'ch', 'seq')
The draws below stay inside these ranges and needn't reach their ends.
All inputs are finite; a program needn't handle non-finite values.
Results may differ from the reference program's by a relative error of at most 0.012.
Values may be sent and summed in bfloat16 or wider, within the bound.
A program may use at most 192 MiB of HBM per device.

```python
import math
import jax
import jax.numpy as jnp
from jax import lax

D = 768
NB = 4
N1 = 512
N2 = 512
SEQS = 1
HB = 768


def draw_stream(key, part):
    key = jax.random.fold_in(key, 7)
    base_key, chan_key, rows_key = jax.random.split(key, 3)
    full_shape = (SEQS, D, N1 * N2)
    column = jnp.arange(D, dtype=jnp.float32) / D
    jitter = jnp.exp(jax.random.uniform(chan_key, (D,), jnp.float32, math.log(0.7), math.log(1.4)))
    channel_scale = (0.2 * jnp.power(10.0, column) * jitter)[:, None]
    base_draw = jnp.clip(jax.random.normal(base_key, full_shape, jnp.float32), -5.0, 5.0)
    row_scale = jnp.exp(jax.random.uniform(rows_key, (SEQS, 1, N1 * N2), jnp.float32, math.log(0.3), math.log(3.0)))
    return jnp.clip(base_draw * channel_scale * row_scale, -40.0, 40.0).astype(jnp.bfloat16)


def shard_levels(own_key, shape, pieces, low, top_value):
    loudness = 1.0
    for dim, parts in pieces:
        draws = jax.random.uniform(jax.random.fold_in(jax.random.fold_in(own_key, 6), dim), (parts,), jnp.float32, low / len(pieces), top_value / len(pieces))
        loudness = loudness * jnp.repeat(jnp.exp(draws), shape[dim] // parts).reshape((-1,) + (1,) * (len(shape) - 1 - dim))
    return loudness


def bell_draw(own_key, shape, scale, most, cuts=(), kind=jnp.bfloat16):
    level = shard_levels(own_key, shape, cuts, -0.22, 0.18) if cuts else 1.0
    values = jax.random.normal(own_key, shape, jnp.float32) * scale * level
    return jnp.minimum(jnp.maximum(values, -most), most).astype(kind)


def setup_inputs(seed: int = 0) -> dict:
    keys = jax.random.split(jax.random.key(seed), 17)
    stream = draw_stream(jax.random.fold_in(keys[16], 71), 0)
    in_weight = bell_draw(keys[1], (D,), 1.0, 4.0, ((0, 4),), jnp.float32)
    in_bias = jnp.clip(jax.random.uniform(keys[2], (D,), jnp.float32, -2.0, 2.0) * shard_levels(keys[2], (D,), ((0, 4),), -0.4, 0.0), -2.0, 2.0)
    out_weight = bell_draw(keys[3], (D,), 1.0, 4.0, ((0, 4),), jnp.float32)
    out_bias = jnp.clip(jax.random.uniform(keys[4], (D,), jnp.float32, -2.0, 2.0) * shard_levels(keys[4], (D,), ((0, 4),), -0.4, 0.0), -2.0, 2.0)
    first_mix = bell_draw(keys[5], (N1, N1), N1 ** -0.5, 0.25)
    twist_in = bell_draw(keys[6], (N1, N2), 1.0, 4.0, ((1, 64),))
    second_mix = bell_draw(keys[7], (N2, N2), N2 ** -0.5, 0.25)
    kernel = bell_draw(keys[8], (D, N1, N2), 1.0, 4.0, ((0, 4), (1, 64)))
    third_mix = bell_draw(keys[9], (N2, N2), N2 ** -0.5, 0.25)
    twist_out = bell_draw(keys[10], (N1, N2), 1.0, 4.0, ((1, 64),))
    fourth_mix = bell_draw(keys[11], (N1, N1), N1 ** -0.5, 0.25)
    norm_gain = jnp.clip(jnp.exp(jax.random.uniform(keys[12], (D,), jnp.float32, math.log(0.5), math.log(2.0))), 0.5, 2.0).astype(jnp.bfloat16)
    gate_weight = bell_draw(keys[13], (NB, D // NB, HB), (D // NB) ** -0.5, 0.4375)
    up_weight = bell_draw(keys[14], (NB, D // NB, HB), (D // NB) ** -0.5, 0.4375)
    down_weight = bell_draw(keys[15], (NB, D // NB, HB), HB ** -0.5, 0.21875)
    return dict(stream=stream, in_weight=in_weight, in_bias=in_bias, out_weight=out_weight, out_bias=out_bias, first_mix=first_mix, twist_in=twist_in, second_mix=second_mix, kernel=kernel, third_mix=third_mix, twist_out=twist_out, fourth_mix=fourth_mix, norm_gain=norm_gain, gate_weight=gate_weight, up_weight=up_weight, down_weight=down_weight)


epsilon = 1e-05

def rounded(array_in):
    return lax.optimization_barrier(array_in.astype(jnp.bfloat16))

def to_wide(array_in):
    return array_in.astype(jnp.float32)

def reference(stream, in_weight, in_bias, out_weight, out_bias, first_mix, twist_in, second_mix, kernel, third_mix, twist_out, fourth_mix, norm_gain, gate_weight, up_weight, down_weight):
    group_width = D // NB
    hidden_part = HB // NB
    stream_rows = stream.transpose(0, 2, 1)
    kernel_rows = kernel.transpose(1, 2, 0)
    down_rows = down_weight.transpose(0, 2, 1)
    blocks = stream_rows.reshape(SEQS, N1, N2, NB, group_width).transpose(3, 0, 1, 2, 4)
    kernel_blocks = kernel_rows.reshape(N1, N2, NB, group_width).transpose(2, 0, 1, 3)
    first_wide = to_wide(first_mix)
    second_wide = to_wide(second_mix)
    third_wide = to_wide(third_mix)
    fourth_wide = to_wide(fourth_mix)
    twist_one = to_wide(twist_in)[None, :, :, None]
    twist_two = to_wide(twist_out)[None, :, :, None]

    def mix_group(operands):
        block_in, kernel_in, gain_in, shift_in, gain_out, shift_out = operands
        source = to_wide(block_in)
        gated_in = rounded(source * jax.nn.sigmoid(source * gain_in + shift_in))
        section_one = rounded(jnp.einsum('ai,sijc->sajc', first_wide, to_wide(gated_in)) * twist_one)
        section_two = rounded(jnp.einsum('bj,sajc->sabc', second_wide, to_wide(section_one)) * to_wide(kernel_in)[None])
        section_three = rounded(jnp.einsum('eb,sabc->saec', third_wide, to_wide(section_two)))
        twisted = rounded(to_wide(section_three) * twist_two)
        returned = rounded(jnp.einsum('ka,saec->skec', fourth_wide, to_wide(twisted)))
        return (source + to_wide(returned) * jax.nn.sigmoid(source * gain_out + shift_out)).astype(jnp.bfloat16)
    mixed_blocks = lax.map(mix_group, (blocks, kernel_blocks, in_weight.reshape(NB, group_width), in_bias.reshape(NB, group_width), out_weight.reshape(NB, group_width), out_bias.reshape(NB, group_width)))
    mixed_all = mixed_blocks.transpose(1, 2, 3, 0, 4).reshape(SEQS * N1 * N2, D)
    rows_block = min(4096, SEQS * N1 * N2)
    gate_wide = to_wide(gate_weight)
    up_wide = to_wide(up_weight)
    down_wide = to_wide(down_rows).reshape(NB, NB, hidden_part, group_width)
    gain_wide = to_wide(norm_gain)

    def feed_forward(block_in):
        source = to_wide(block_in)
        square_mean = lax.optimization_barrier(jnp.mean(source * source, axis=-1, keepdims=True))
        normed = rounded(source * lax.rsqrt(square_mean + epsilon) * gain_wide)
        split_in = to_wide(normed).reshape(-1, NB, group_width)
        gate_value = jnp.einsum('tnc,nch->tnh', split_in, gate_wide)
        up_value = jnp.einsum('tnc,nch->tnh', split_in, up_wide)
        hidden = rounded(jax.nn.silu(gate_value) * up_value)
        spread = to_wide(hidden).reshape(-1, NB, NB, hidden_part)
        down_value = jnp.einsum('tnkm,knmq->tkq', spread, down_wide).reshape(-1, D)
        return (source + down_value).astype(jnp.bfloat16)
    outcome = lax.map(feed_forward, mixed_all.reshape(-1, rows_block, D))
    return outcome.reshape(SEQS, N1 * N2, D).transpose(0, 2, 1)
```

```python
import jax
import jax.numpy as jnp
from jax import lax
from jax.experimental import pallas as pl
from jax.experimental.pallas import tpu as pltpu
from jax.sharding import PartitionSpec as P

epsilon = 1e-05
MESH = pl.DeviceIdType.MESH
NZ, NX, NY = 8, 4, 2
NXY = NX * NY
NS = NZ * NXY
NC = 4
BF = jnp.bfloat16


def to_wide(array_in):
    return array_in.astype(jnp.float32)


def each_peer(me, core, act):
    z, x, y = lax.div(me, NXY), lax.rem(lax.div(me, NY), NX), lax.rem(me, NY)
    layers = [lax.rem(z + (3 + 2 * core) * low, NZ) * NXY for low in range(NZ)]

    def peer(high, low):
        new_x = lax.rem(x + (high + low) * (1 + 2 * core), NX)
        new_y = lax.rem(y + lax.div(high, NX) + low // NX, NY)
        return layers[low] + new_x * NY + new_y

    for low in range(1, NZ):
        act(peer(jnp.int32(0), low))

    def row(high, carry):
        for low in range(NZ):
            act(peer(high, low))
        return carry

    lax.fori_loop(1, NXY, row, 0)


def turned_dot(left, right):
    return lax.dot_general(left, right, (((1,), (1,)), ((), ())), preferred_element_type=jnp.float32)


def dot(left, right):
    return jnp.dot(left, right, preferred_element_type=jnp.float32)


def layer_kernel(
    slope_in,
    shift_in,
    slope_out,
    shift_out,
    gain_ref,
    twist_in_ref,
    twist_out_ref,
    stream_any,
    kernel_any,
    first_any,
    second_any,
    third_any,
    fourth_any,
    gate_any,
    up_any,
    down_any,
    out_ref,
    stream_ref,
    kernel_ref,
    mixes,
    gate_ref,
    up_ref,
    down_ref,
    param_ref,
    gains,
    twist_ref,
    gated,
    send,
    got,
    tables,
    table_in,
    table_out,
    held,
    back,
    home,
    wide_home,
    half,
    own_gate,
    mixed,
    turned,
    chosen,
    normed,
    hidden,
    leaving,
    load_sem,
    send_sem,
    got_sem,
    twist_sem,
    home_sem,
    half_sem,
    swap_sem,
    out_sem,
    plane_sem,
    side_sem,
):
    me = lax.axis_index("seq")
    ch = lax.axis_index("ch")
    core = lax.rem(ch, 2)
    side = lax.div(ch, 2)
    across = (1 - side) * 2 + core
    partner = side * 2 + 1 - core
    my_z, my_xy = lax.div(me, NXY), lax.rem(me, NXY)
    few = got.shape[0]

    loads = [
        pltpu.make_async_copy(source, target, load_sem.at[i])
        for i, (source, target) in enumerate(
            (
                (stream_any, stream_ref),
                (kernel_any, kernel_ref),
                (first_any, mixes.at[0]),
                (second_any, mixes.at[1]),
                (third_any, mixes.at[2]),
                (fourth_any, mixes.at[3]),
                (gate_any, gate_ref),
                (up_any, up_ref),
                (down_any, down_ref),
            )
        )
    ]
    for load in loads:
        load.start()

    barrier = pltpu.get_barrier_semaphore()

    columns = [lax.rem(my_z + 3 * q, NZ) * NXY + my_xy for q in range(1, NZ)]
    planes = [my_z * NXY + lax.rem(my_xy + q, NXY) for q in range(1, NXY)]
    for peer in columns + planes:
        pl.semaphore_signal(barrier, 1, device_id={"seq": peer}, device_id_type=MESH)
    for q in range(1, NC):
        pl.semaphore_signal(barrier, 1, device_id={"ch": lax.rem(ch + q, NC)}, device_id_type=MESH)

    def spread(row):
        return jnp.broadcast_to(row, (128, row.shape[1])).T

    for i, row in enumerate((slope_in, shift_in, slope_out, shift_out)):
        param_ref[i] = spread(row[...])
    twist_ref[...] = jnp.concatenate(
        [to_wide(twist_in_ref[...]), to_wide(twist_out_ref[...])], axis=0
    ).astype(BF)

    def pack(c):
        rows = slice(64 * c, 64 * c + 64)
        slope, shift = param_ref[0, rows, :], param_ref[1, rows, :]

        def one(i, carry):
            for q in range(4):
                lanes = pl.ds(pl.multiple_of(i * 512 + q * 128, 128), 128)
                value = to_wide(stream_ref[rows, lanes])
                value = value * jax.nn.sigmoid(value * slope + shift)
                gated[q, pl.ds(i, 64, stride=8), :] = value
            return carry

        lax.fori_loop(0, 8, one, 0)
        for q in range(4):
            lanes = slice(128 * q, 128 * q + 128)
            top = gated[q].reshape(64, 8, 128)
            low = to_wide(kernel_ref[rows, :, lanes])
            send[c, :, :, lanes] = jnp.concatenate([top, low], axis=1).astype(BF)

    def send_lines(c):
        def one(peer):
            pltpu.make_async_remote_copy(
                src_ref=send.at[c, peer],
                dst_ref=got.at[c, me],
                send_sem=send_sem.at[1],
                recv_sem=got_sem.at[c],
                device_id={"seq": peer},
                device_id_type=MESH,
            ).start()

        each_peer(me, core, one)
        got[c, me] = send[c, me]

    def bytes_of(ref, sem):
        pltpu.make_async_copy(ref, ref, sem).wait()

    loads[0].wait()
    loads[1].wait()
    pack(0)
    pl.semaphore_wait(barrier, NZ - 1 + NXY - 1 + NC - 1)
    for peer in planes:
        pl.semaphore_signal(plane_sem, 1, device_id={"seq": peer}, device_id_type=MESH)

    lanes = pl.ds(pl.multiple_of(ch * 128, 128), 128)
    for peer in columns:
        pltpu.make_async_remote_copy(
            src_ref=twist_ref.at[:, lanes],
            dst_ref=tables.at[ch, my_xy, my_z],
            send_sem=send_sem.at[0],
            recv_sem=twist_sem.at[0],
            device_id={"seq": peer},
            device_id_type=MESH,
        ).start()
    tables[ch, my_xy, my_z] = twist_ref[:, lanes]
    pl.semaphore_wait(plane_sem, NXY - 1)
    pl.semaphore_signal(side_sem, 1, device_id={"ch": across}, device_id_type=MESH)
    send_lines(0)
    pack(1)
    send_lines(1)
    bytes_of(tables.at[0, 0, pl.ds(0, NZ - 1)], twist_sem.at[0])
    for peer in planes:
        pltpu.make_async_remote_copy(
            src_ref=tables.at[ch, my_xy],
            dst_ref=tables.at[ch, my_xy],
            send_sem=send_sem.at[4],
            recv_sem=twist_sem.at[1],
            device_id={"seq": peer},
            device_id_type=MESH,
        ).start()
    pack(2)
    send_lines(2)
    bytes_of(tables.at[0, pl.ds(0, NXY - 1)], twist_sem.at[1])
    for q in range(1, NC):
        pltpu.make_async_remote_copy(
            src_ref=tables.at[ch],
            dst_ref=tables.at[ch],
            send_sem=send_sem.at[5],
            recv_sem=twist_sem.at[2],
            device_id={"ch": lax.rem(ch + q, NC)},
            device_id_type=MESH,
        ).start()
    for i in range(8):
        for e in range(2):
            lanes = pl.ds(pl.multiple_of(i * 512 + 256 * (1 - side) + 128 * e, 128), 128)
            pltpu.make_async_remote_copy(
                src_ref=stream_ref.at[:, lanes],
                dst_ref=half.at[side, :, pl.ds(e * 1024 + i * 128, 128)],
                send_sem=send_sem.at[2],
                recv_sem=half_sem.at[0],
                device_id={"ch": across},
                device_id_type=MESH,
            ).start()
    pltpu.make_async_remote_copy(
        src_ref=param_ref.at[pl.ds(2, 2)],
        dst_ref=own_gate.at[side],
        send_sem=send_sem.at[3],
        recv_sem=half_sem.at[1],
        device_id={"ch": across},
        device_id_type=MESH,
    ).start()

    for i in range(8):
        for e in range(2):
            lanes = pl.ds(pl.multiple_of(i * 512 + 256 * side + 128 * e, 128), 128)
            half[side, :, e * 1024 + i * 128 : e * 1024 + i * 128 + 128] = stream_ref[:, lanes]
    own_gate[side] = param_ref[2:4]
    gains[...] = spread(to_wide(gain_ref[...]).reshape(1, 768))

    for load in loads[2:]:
        load.wait()

    def choose(n, carry):
        for w, source in enumerate((gate_ref, up_ref)):
            turned[...] = to_wide(source[n]).T.astype(BF)
            for j, k in enumerate((ch, across)):
                chosen[n, (2 * j + w) * 192 : (2 * j + w + 1) * 192, :] = turned[
                    pl.ds(pl.multiple_of(k * 192, 192), 192), :
                ]
        return carry

    lax.fori_loop(0, NC, choose, 0)

    bytes_of(tables.at[pl.ds(0, NC - 1)], twist_sem.at[2])
    for q in range(NC):
        rows = slice(q * 128, (q + 1) * 128)
        part = to_wide(tables[q])
        part = jnp.concatenate([part[:, z] for z in range(NZ)], axis=0)
        part = part.reshape(NS, 2, 8, 128)
        table_in[rows, :] = part[:, 0].reshape(NS * 8, 128).T
        table_out[rows, :] = part[:, 1].reshape(NS * 8, 128).T

    def arrive(c):
        bytes_of(got.at[c, pl.ds(0, NS - 1)], got_sem.at[c])

    def mix(c):
        block = to_wide(got[c]).reshape(NS, 2, 8, 512)
        lines = block[:, 0].reshape(512, 512).astype(BF)
        value = dot(mixes[0], lines)
        value = (value * table_in[...]).astype(BF)
        value = turned_dot(value, mixes[1])
        block = to_wide(got[c]).reshape(NS, 2, 8, 512)
        value = (value * block[:, 1].reshape(512, 512)).astype(BF)
        value = turned_dot(value, mixes[2])
        value = (to_wide(value.astype(BF)) * table_out[...]).astype(BF)
        return dot(mixes[3], value)

    def quarter(value, h, e):
        start = 256 * h + 128 * e
        return value[:, start : start + 128].reshape(NS, 8, 128)

    def send_back(step, same=True, far=True):
        def one(peer, near):
            to_side, to_ch = (side, ch) if near else (1 - side, across)
            pltpu.make_async_remote_copy(
                src_ref=back.at[step, to_side, peer],
                dst_ref=home.at[step, side, me],
                send_sem=send_sem.at[6],
                recv_sem=home_sem.at[step, 0 if near else 1],
                device_id={"seq": peer, "ch": to_ch},
                device_id_type=MESH,
            ).start()

        def both(peer):
            if same:
                one(peer, True)
            if far:
                one(peer, False)

        each_peer(me, core, both)
        if far:
            one(me, False)
        if same:
            home[step, side, me] = back[step, side, me]

    def widen(step):
        bytes_of(home.at[step, 0, pl.ds(0, NS - 1)], home_sem.at[step, 0])
        bytes_of(home.at[step, 0], home_sem.at[step, 1])
        for y in range(2):
            wide_home[step, y] = to_wide(home[step, y]).reshape(NS * 16, 128)

    def gate_out(c, e, i):
        step, row = (0, e * 8 + i) if c == 0 else (1 + e, (c - 1) * 8 + i)
        rows = slice(64 * c, 64 * c + 64)
        lanes = slice(e * 1024 + i * 128, e * 1024 + i * 128 + 128)

        def one(y, carry):
            slope, shift = own_gate[y, 0, rows, :], own_gate[y, 1, rows, :]
            value = to_wide(half[y, rows, lanes])
            came = wide_home[step, y, pl.ds(row, 64, stride=16), :]
            value = value + came * jax.nn.sigmoid(value * slope + shift)
            mixed[core, y, rows, lanes] = value.astype(BF)
            return carry

        lax.fori_loop(0, 2, one, 0)

    def swap(rows, tokens, sem):
        part = mixed.at[core, :, rows, tokens]
        pltpu.make_async_remote_copy(
            src_ref=part,
            dst_ref=part,
            send_sem=send_sem.at[8],
            recv_sem=sem,
            device_id={"ch": partner},
            device_id_type=MESH,
        ).start()

    arrive(0)
    value = mix(0)
    for h in range(2):
        back[0, h] = jnp.concatenate([quarter(value, h, 0), quarter(value, h, 1)], axis=1).astype(
            BF
        )
    arrive(1)
    held[...] = mix(1)
    pl.semaphore_wait(side_sem, 1)
    send_back(0, same=False)
    arrive(2)
    send_back(0, far=False)
    value = mix(2)
    for e in range(2):
        for h in range(2):
            back[1 + e, h] = jnp.concatenate(
                [quarter(held, h, e), quarter(value, h, e)], axis=1
            ).astype(BF)
    send_back(1)
    bytes_of(half.at[0], half_sem.at[0])
    bytes_of(own_gate.at[0], half_sem.at[1])
    widen(0)
    for e in range(2):
        for i in range(8):
            gate_out(0, e, i)
    swap(pl.ds(0, 64), pl.ds(0, 2048), swap_sem.at[0])
    send_back(2)

    def normalize(start, size):
        tokens = slice(start, start + size)
        slot = tokens
        total = jnp.zeros((1, size), jnp.float32)
        for n in range(NC):
            value = to_wide(mixed[n % 2, n // 2, :, tokens])
            total = total + jnp.sum(value * value, axis=0, keepdims=True)
        inverse = lax.rsqrt(total / 768.0 + epsilon)
        for n in range(NC):
            value = to_wide(mixed[n % 2, n // 2, :, tokens])
            gain = gains[192 * n : 192 * n + 192, :]
            gain = jnp.concatenate([gain] * (size // 128), axis=1)
            normed[192 * n : 192 * n + 192, slot] = (value * inverse * gain).astype(BF)

    def block(start, size, j):
        tokens = slice(start, start + size)
        slot = tokens
        for n in range(NC):
            wide = dot(
                chosen[n, 384 * j : 384 * j + 384, :], normed[192 * n : 192 * n + 192, slot]
            )
            gate, up = wide[:192], wide[192:]
            hidden[192 * n : 192 * n + 192, :size] = (gate / (1.0 + jnp.exp(-gate)) * up).astype(BF)
        value = dot(down_ref[(ch, across)[j]], hidden[:, :size])
        return (to_wide(mixed[core, (side, 1 - side)[j], :, tokens]) + value).astype(BF)

    def place(token):
        start = 512 * (token % 1024 // 128) + 256 * side + 128 * (token // 1024)
        return pl.ds(pl.multiple_of(start, 128), 128)

    def across_block(start, size):
        leaving[:, start : start + size] = block(start, size, 1)
        for token in range(start, start + size, 128):
            pltpu.make_async_remote_copy(
                src_ref=leaving.at[:, pl.ds(token, 128)],
                dst_ref=out_ref.at[:, place(token)],
                send_sem=send_sem.at[9],
                recv_sem=out_sem,
                device_id={"ch": across},
                device_id_type=MESH,
            ).start()

    def own_block(start, size):
        value = block(start, size, 0)
        for i in range(0, size, 128):
            out_ref[:, place(start + i)] = value[:, i : i + 128]

    for e, size, first in ((0, 512, 1), (1, 256, 3)):
        widen(1 + e)
        starts = range(1024 * e, 1024 * e + 1024, size)
        for t, start in enumerate(starts):
            for i in range(start % 1024 // 128, (start % 1024 + size) // 128):
                gate_out(1, e, i)
                gate_out(2, e, i)
            swap(pl.ds(64, 128), pl.ds(start, size), swap_sem.at[first + t])
        if e == 0:
            bytes_of(mixed.at[0, :, pl.ds(0, 64)], swap_sem.at[0])
        for t, start in enumerate(starts):
            bytes_of(mixed.at[0, :, pl.ds(64, 128), pl.ds(start, size)], swap_sem.at[first + t])
            normalize(start, size)
            across_block(start, size)

    for start in range(0, 2048, 512):
        own_block(start, 512)

    bytes_of(leaving, out_sem)
    bytes_of(leaving, send_sem.at[9])
    bytes_of(mixed.at[0], send_sem.at[8])
    for step in range(3):
        bytes_of(home.at[step, 0, pl.ds(0, NS - 1)], send_sem.at[6])
        bytes_of(home.at[step, 0], send_sem.at[6])
    for c in range(few):
        bytes_of(got.at[c, pl.ds(0, NS - 1)], send_sem.at[1])
    bytes_of(tables.at[0, 0, pl.ds(0, NZ - 1)], send_sem.at[0])
    bytes_of(tables.at[0, pl.ds(0, NXY - 1)], send_sem.at[4])
    bytes_of(tables.at[pl.ds(0, NC - 1)], send_sem.at[5])
    bytes_of(half.at[0], send_sem.at[2])
    bytes_of(own_gate.at[0], send_sem.at[3])


def local(
    stream,
    in_weight,
    in_bias,
    out_weight,
    out_bias,
    first_mix,
    twist_in,
    second_mix,
    kernel,
    third_mix,
    twist_out,
    fourth_mix,
    norm_gain,
    gate_weight,
    up_weight,
    down_weight,
):
    _, width, tokens = stream.shape
    few = width // NS
    fast = pl.BlockSpec(memory_space=pltpu.VMEM)
    slow = pl.BlockSpec(memory_space=pl.ANY)
    wide, half = jnp.float32, BF
    dma = pltpu.SemaphoreType.DMA
    out = pl.pallas_call(
        layer_kernel,
        out_shape=pltpu.VMEM((width, tokens), BF),
        in_specs=[fast] * 7 + [slow] * 9,
        out_specs=fast,
        scratch_shapes=[
            pltpu.VMEM((width, tokens), half),
            pltpu.VMEM(kernel.shape, half),
            pltpu.VMEM((4, 512, 512), half),
            pltpu.VMEM(gate_weight.shape, half),
            pltpu.VMEM(up_weight.shape, half),
            pltpu.VMEM(down_weight.shape, half),
            pltpu.VMEM((4, width, 128), wide),
            pltpu.VMEM((4 * width, 128), wide),
            pltpu.VMEM((16, 512), half),
            pltpu.VMEM((4, 512, 128), wide),
            pltpu.VMEM((few, NS, 16, 512), half),
            pltpu.VMEM((few, NS, 16, 512), half),
            pltpu.VMEM((NC, NXY, NZ, 16, 128), half),
            pltpu.VMEM((512, 512), wide),
            pltpu.VMEM((512, 512), wide),
            pltpu.VMEM((512, 512), wide),
            pltpu.VMEM((3, 2, NS, 16, 128), half),
            pltpu.VMEM((3, 2, NS, 16, 128), half),
            pltpu.VMEM((3, 2, NS * 16, 128), wide),
            pltpu.VMEM((2, width, tokens // 2), half),
            pltpu.VMEM((2, 2, width, 128), wide),
            pltpu.VMEM((2, 2, width, tokens // 2), half),
            pltpu.VMEM((4 * width, width), half),
            pltpu.VMEM((NC, 4 * width, width), half),
            pltpu.VMEM((4 * width, tokens // 2), half),
            pltpu.VMEM((4 * width, 512), half),
            pltpu.VMEM((width, tokens // 2), half),
            dma((9,)),
            dma((10,)),
            dma((few,)),
            dma((3,)),
            dma((3, 2)),
            dma((2,)),
            dma((7,)),
            dma,
            pltpu.SemaphoreType.REGULAR,
            pltpu.SemaphoreType.REGULAR,
        ],
        compiler_params=pltpu.CompilerParams(
            collective_id=0, has_side_effects=True, vmem_limit_bytes=58 * 2**20
        ),
    )(
        in_weight.reshape(1, width),
        in_bias.reshape(1, width),
        out_weight.reshape(1, width),
        out_bias.reshape(1, width),
        norm_gain,
        twist_in.T,
        twist_out.T,
        stream[0],
        kernel,
        first_mix,
        second_mix,
        third_mix,
        fourth_mix,
        gate_weight,
        up_weight,
        down_weight,
    )
    return out[None]


def solution(mesh):
    in_specs = (
        P(None, "ch", "seq"),
        P("ch"),
        P("ch"),
        P("ch"),
        P("ch"),
        P(),
        P(None, "seq"),
        P(),
        P("ch", "seq", None),
        P(),
        P(None, "seq"),
        P(),
        P(),
        P(),
        P(),
        P(),
    )
    out_specs = P(None, "ch", "seq")
    return jax.shard_map(local, mesh=mesh, in_specs=in_specs, out_specs=out_specs, check_vma=False)
```

```python
import jax
import jax.numpy as jnp
from jax import lax
from jax.experimental import pallas as pl
from jax.experimental.pallas import tpu as pltpu
from jax.sharding import PartitionSpec as P

epsilon = 1e-05
MESH = pl.DeviceIdType.MESH
NZ, NX, NY = 8, 4, 2
NXY = NX * NY
NS = NZ * NXY
NC = 4
BF = jnp.bfloat16


def to_wide(array_in):
    return array_in.astype(jnp.float32)


def each_peer(me, core, act):
    z, x, y = lax.div(me, NXY), lax.rem(lax.div(me, NY), NX), lax.rem(me, NY)
    layers = [lax.rem(z + (3 + 2 * core) * low, NZ) * NXY for low in range(NZ)]

    def peer(high, low):
        new_x = lax.rem(x + (high + low) * (1 + 2 * core), NX)
        new_y = lax.rem(y + lax.div(high, NX) + low // NX, NY)
        return layers[low] + new_x * NY + new_y

    for low in range(1, NZ):
        act(peer(jnp.int32(0), low))

    def row(high, carry):
        for low in range(NZ):
            act(peer(high, low))
        return carry

    lax.fori_loop(1, NXY, row, 0)


def gate_by(value, score):
    value = 0.5 * value
    return value + value * jnp.tanh(0.5 * score)


def turned_dot(left, right):
    return lax.dot_general(left, right, (((1,), (1,)), ((), ())), preferred_element_type=jnp.float32)


def dot(left, right):
    return jnp.dot(left, right, preferred_element_type=jnp.float32)


def layer_kernel(
    slope_in,
    shift_in,
    slope_out,
    shift_out,
    gain_ref,
    twist_in_ref,
    twist_out_ref,
    stream_any,
    kernel_any,
    first_any,
    second_any,
    third_any,
    fourth_any,
    gate_any,
    up_any,
    down_any,
    out_ref,
    stream_ref,
    kernel_ref,
    mixes,
    gate_ref,
    up_ref,
    down_ref,
    param_ref,
    gains,
    twist_ref,
    gated,
    send,
    got,
    tables,
    table_in,
    table_out,
    held,
    back,
    home,
    wide_home,
    half,
    own_gate,
    mixed,
    turned,
    chosen,
    normed,
    hidden,
    leaving,
    load_sem,
    send_sem,
    got_sem,
    twist_sem,
    home_sem,
    half_sem,
    swap_sem,
    out_sem,
    plane_sem,
    side_sem,
):
    me = lax.axis_index("seq")
    ch = lax.axis_index("ch")
    core = lax.rem(ch, 2)
    side = lax.div(ch, 2)
    across = (1 - side) * 2 + core
    partner = side * 2 + 1 - core
    my_z, my_xy = lax.div(me, NXY), lax.rem(me, NXY)
    few = got.shape[0]

    loads = [
        pltpu.make_async_copy(source, target, load_sem.at[i])
        for i, (source, target) in enumerate(
            (
                (stream_any, stream_ref),
                (kernel_any, kernel_ref),
                (first_any, mixes.at[0]),
                (second_any, mixes.at[1]),
                (third_any, mixes.at[2]),
                (fourth_any, mixes.at[3]),
                (gate_any, gate_ref),
                (up_any, up_ref),
                (down_any, down_ref),
            )
        )
    ]
    for load in loads:
        load.start()

    barrier = pltpu.get_barrier_semaphore()

    columns = [lax.rem(my_z + 3 * q, NZ) * NXY + my_xy for q in range(1, NZ)]
    planes = [my_z * NXY + lax.rem(my_xy + q, NXY) for q in range(1, NXY)]
    for peer in columns + planes:
        pl.semaphore_signal(barrier, 1, device_id={"seq": peer}, device_id_type=MESH)
    for q in range(1, NC):
        pl.semaphore_signal(barrier, 1, device_id={"ch": lax.rem(ch + q, NC)}, device_id_type=MESH)

    def spread(row):
        return jnp.broadcast_to(row, (128, row.shape[1])).T

    for i, row in enumerate((slope_in, shift_in, slope_out, shift_out)):
        param_ref[i] = spread(row[...])
    twist_ref[...] = jnp.concatenate(
        [to_wide(twist_in_ref[...]), to_wide(twist_out_ref[...])], axis=0
    ).astype(BF)

    def pack(c):
        rows = slice(64 * c, 64 * c + 64)
        slope, shift = param_ref[0, rows, :], param_ref[1, rows, :]

        def one(i, carry):
            for q in range(4):
                lanes = pl.ds(pl.multiple_of(i * 512 + q * 128, 128), 128)
                value = to_wide(stream_ref[rows, lanes])
                value = gate_by(value, value * slope + shift)
                gated[q, pl.ds(i, 64, stride=8), :] = value
            return carry

        lax.fori_loop(0, 8, one, 0)
        for q in range(4):
            lanes = slice(128 * q, 128 * q + 128)
            top = gated[q].reshape(64, 8, 128)
            low = to_wide(kernel_ref[rows, :, lanes])
            send[c, :, :, lanes] = jnp.concatenate([top, low], axis=1).astype(BF)

    def send_lines(c):
        def one(peer):
            pltpu.make_async_remote_copy(
                src_ref=send.at[c, peer],
                dst_ref=got.at[c, me],
                send_sem=send_sem.at[1],
                recv_sem=got_sem.at[c],
                device_id={"seq": peer},
                device_id_type=MESH,
            ).start()

        each_peer(me, core, one)
        got[c, me] = send[c, me]

    def bytes_of(ref, sem):
        pltpu.make_async_copy(ref, ref, sem).wait()

    loads[0].wait()
    loads[1].wait()
    pack(0)
    pl.semaphore_wait(barrier, NZ - 1 + NXY - 1 + NC - 1)
    for peer in planes:
        pl.semaphore_signal(plane_sem, 1, device_id={"seq": peer}, device_id_type=MESH)

    lanes = pl.ds(pl.multiple_of(ch * 128, 128), 128)
    for peer in columns:
        pltpu.make_async_remote_copy(
            src_ref=twist_ref.at[:, lanes],
            dst_ref=tables.at[ch, my_xy, my_z],
            send_sem=send_sem.at[0],
            recv_sem=twist_sem.at[0],
            device_id={"seq": peer},
            device_id_type=MESH,
        ).start()
    tables[ch, my_xy, my_z] = twist_ref[:, lanes]
    pl.semaphore_wait(plane_sem, NXY - 1)
    pl.semaphore_signal(side_sem, 1, device_id={"ch": across}, device_id_type=MESH)
    send_lines(0)
    pack(1)
    send_lines(1)
    bytes_of(tables.at[0, 0, pl.ds(0, NZ - 1)], twist_sem.at[0])
    for peer in planes:
        pltpu.make_async_remote_copy(
            src_ref=tables.at[ch, my_xy],
            dst_ref=tables.at[ch, my_xy],
            send_sem=send_sem.at[4],
            recv_sem=twist_sem.at[1],
            device_id={"seq": peer},
            device_id_type=MESH,
        ).start()
    pack(2)
    send_lines(2)
    bytes_of(tables.at[0, pl.ds(0, NXY - 1)], twist_sem.at[1])
    for q in range(1, NC):
        pltpu.make_async_remote_copy(
            src_ref=tables.at[ch],
            dst_ref=tables.at[ch],
            send_sem=send_sem.at[5],
            recv_sem=twist_sem.at[2],
            device_id={"ch": lax.rem(ch + q, NC)},
            device_id_type=MESH,
        ).start()
    for i in range(8):
        for e in range(2):
            lanes = pl.ds(pl.multiple_of(i * 512 + 256 * (1 - side) + 128 * e, 128), 128)
            pltpu.make_async_remote_copy(
                src_ref=stream_ref.at[:, lanes],
                dst_ref=half.at[side, :, pl.ds(e * 1024 + i * 128, 128)],
                send_sem=send_sem.at[2],
                recv_sem=half_sem.at[0],
                device_id={"ch": across},
                device_id_type=MESH,
            ).start()
    pltpu.make_async_remote_copy(
        src_ref=param_ref.at[pl.ds(2, 2)],
        dst_ref=own_gate.at[side],
        send_sem=send_sem.at[3],
        recv_sem=half_sem.at[1],
        device_id={"ch": across},
        device_id_type=MESH,
    ).start()

    for i in range(8):
        for e in range(2):
            lanes = pl.ds(pl.multiple_of(i * 512 + 256 * side + 128 * e, 128), 128)
            half[side, :, e * 1024 + i * 128 : e * 1024 + i * 128 + 128] = stream_ref[:, lanes]
    own_gate[side] = param_ref[2:4]
    gains[...] = spread(to_wide(gain_ref[...]).reshape(1, 768))

    for load in loads[2:]:
        load.wait()

    def choose(n, carry):
        for w, source in enumerate((gate_ref, up_ref)):
            turned[...] = to_wide(source[n]).T.astype(BF)
            for j, k in enumerate((ch, across)):
                chosen[n, (2 * j + w) * 192 : (2 * j + w + 1) * 192, :] = turned[
                    pl.ds(pl.multiple_of(k * 192, 192), 192), :
                ]
        return carry

    lax.fori_loop(0, NC, choose, 0)

    bytes_of(tables.at[pl.ds(0, NC - 1)], twist_sem.at[2])
    for q in range(NC):
        rows = slice(q * 128, (q + 1) * 128)
        part = to_wide(tables[q])
        part = jnp.concatenate([part[:, z] for z in range(NZ)], axis=0)
        part = part.reshape(NS, 2, 8, 128)
        table_in[rows, :] = part[:, 0].reshape(NS * 8, 128).T
        table_out[rows, :] = part[:, 1].reshape(NS * 8, 128).T

    def arrive(c):
        bytes_of(got.at[c, pl.ds(0, NS - 1)], got_sem.at[c])

    def mix(c):
        block = to_wide(got[c]).reshape(NS, 2, 8, 512)
        lines = block[:, 0].reshape(512, 512).astype(BF)
        value = dot(mixes[0], lines)
        value = (value * table_in[...]).astype(BF)
        value = turned_dot(value, mixes[1])
        block = to_wide(got[c]).reshape(NS, 2, 8, 512)
        value = (value * block[:, 1].reshape(512, 512)).astype(BF)
        value = turned_dot(value, mixes[2])
        value = (to_wide(value.astype(BF)) * table_out[...]).astype(BF)
        return dot(mixes[3], value)

    def quarter(value, h, e):
        start = 256 * h + 128 * e
        return value[:, start : start + 128].reshape(NS, 8, 128)

    def far_copy(step, peer):
        return pltpu.make_async_remote_copy(
            src_ref=back.at[step, 1 - side, peer],
            dst_ref=home.at[step, side, me],
            send_sem=send_sem.at[6],
            recv_sem=home_sem.at[step, 1],
            device_id={"seq": peer, "ch": across},
            device_id_type=MESH,
        )

    def send_back(step, same=True, far=True):
        def one(peer, near):
            to_side, to_ch = (side, ch) if near else (1 - side, across)
            pltpu.make_async_remote_copy(
                src_ref=back.at[step, to_side, peer],
                dst_ref=home.at[step, side, me],
                send_sem=send_sem.at[6],
                recv_sem=home_sem.at[step, 0 if near else 1],
                device_id={"seq": peer, "ch": to_ch},
                device_id_type=MESH,
            ).start()

        def both(peer):
            if same:
                one(peer, True)
            if far:
                one(peer, False)

        each_peer(me, core, both)
        if far:
            far_copy(step, me).start()
        if same:
            home[step, side, me] = back[step, side, me]

    def send_last(late):
        def one(peer):
            to_side = lax.rem(lax.div(peer, NXY) + lax.div(peer, NY) + peer + late, 2)
            pltpu.make_async_remote_copy(
                src_ref=back.at[2, to_side, peer],
                dst_ref=home.at[2, side, me],
                send_sem=send_sem.at[6],
                recv_sem=home_sem.at[2, lax.rem(to_side + side, 2)],
                device_id={"seq": peer, "ch": to_side * 2 + core},
                device_id_type=MESH,
            ).start()

        each_peer(me, core, one)

    def widen(step):
        bytes_of(home.at[step, 0, pl.ds(0, NS - 1)], home_sem.at[step, 0])
        bytes_of(home.at[step, 0], home_sem.at[step, 1])
        for y in range(2):
            wide_home[step, y] = to_wide(home[step, y]).reshape(NS * 16, 128)

    def gate_out(c, e, i):
        step, row = (0, e * 8 + i) if c == 0 else (1 + e, (c - 1) * 8 + i)
        rows = slice(64 * c, 64 * c + 64)
        lanes = slice(e * 1024 + i * 128, e * 1024 + i * 128 + 128)

        def one(y, carry):
            slope, shift = own_gate[y, 0, rows, :], own_gate[y, 1, rows, :]
            value = to_wide(half[y, rows, lanes])
            came = wide_home[step, y, pl.ds(row, 64, stride=16), :]
            value = value + gate_by(came, value * slope + shift)
            mixed[core, y, rows, lanes] = value.astype(BF)
            return carry

        lax.fori_loop(0, 2, one, 0)

    def swap(rows, tokens, sem):
        part = mixed.at[core, :, rows, tokens]
        pltpu.make_async_remote_copy(
            src_ref=part,
            dst_ref=part,
            send_sem=send_sem.at[8],
            recv_sem=sem,
            device_id={"ch": partner},
            device_id_type=MESH,
        ).start()

    arrive(0)
    value = mix(0)
    for h in range(2):
        back[0, h] = jnp.concatenate([quarter(value, h, 0), quarter(value, h, 1)], axis=1).astype(
            BF
        )
    arrive(1)
    held[...] = mix(1)
    pl.semaphore_wait(side_sem, 1)
    send_back(0, same=False)
    arrive(2)
    send_back(0, far=False)
    value = mix(2)
    for e in range(2):
        for h in range(2):
            back[1 + e, h] = jnp.concatenate(
                [quarter(held, h, e), quarter(value, h, e)], axis=1
            ).astype(BF)
    send_back(1)
    bytes_of(half.at[0], half_sem.at[0])
    bytes_of(own_gate.at[0], half_sem.at[1])
    widen(0)
    for e in range(2):
        for i in range(8):
            gate_out(0, e, i)
    swap(pl.ds(0, 64), pl.ds(0, 2048), swap_sem.at[0])
    send_last(0)
    far_copy(2, me).start()
    send_last(1)
    home[2, side, me] = back[2, side, me]

    def normalize(start, size):
        tokens = slice(start, start + size)
        slot = tokens
        total = jnp.zeros((1, size), jnp.float32)
        for n in range(NC):
            value = to_wide(mixed[n % 2, n // 2, :, tokens])
            total = total + jnp.sum(value * value, axis=0, keepdims=True)
        inverse = lax.rsqrt(total / 768.0 + epsilon)
        for n in range(NC):
            value = to_wide(mixed[n % 2, n // 2, :, tokens])
            gain = gains[192 * n : 192 * n + 192, :]
            gain = jnp.concatenate([gain] * (size // 128), axis=1)
            normed[192 * n : 192 * n + 192, slot] = (value * inverse * gain).astype(BF)

    def block(start, size, j):
        tokens = slice(start, start + size)
        slot = tokens
        for n in range(NC):
            wide = dot(
                chosen[n, 384 * j : 384 * j + 384, :], normed[192 * n : 192 * n + 192, slot]
            )
            gate, up = wide[:192], wide[192:]
            hidden[192 * n : 192 * n + 192, :size] = (gate_by(gate, gate) * up).astype(BF)
        value = dot(down_ref[(ch, across)[j]], hidden[:, :size])
        return (to_wide(mixed[core, (side, 1 - side)[j], :, tokens]) + value).astype(BF)

    def place(token):
        start = 512 * (token % 1024 // 128) + 256 * side + 128 * (token // 1024)
        return pl.ds(pl.multiple_of(start, 128), 128)

    def across_block(start, size):
        leaving[:, start : start + size] = block(start, size, 1)
        for token in range(start, start + size, 128):
            pltpu.make_async_remote_copy(
                src_ref=leaving.at[:, pl.ds(token, 128)],
                dst_ref=out_ref.at[:, place(token)],
                send_sem=send_sem.at[9],
                recv_sem=out_sem,
                device_id={"ch": across},
                device_id_type=MESH,
            ).start()

    def own_block(start, size):
        value = block(start, size, 0)
        for i in range(0, size, 128):
            out_ref[:, place(start + i)] = value[:, i : i + 128]

    for e, size, first in ((0, 512, 1), (1, 256, 3)):
        widen(1 + e)
        starts = range(1024 * e, 1024 * e + 1024, size)
        for t, start in enumerate(starts):
            for i in range(start % 1024 // 128, (start % 1024 + size) // 128):
                gate_out(1, e, i)
                gate_out(2, e, i)
            swap(pl.ds(64, 128), pl.ds(start, size), swap_sem.at[first + t])
        if e == 0:
            bytes_of(mixed.at[0, :, pl.ds(0, 64)], swap_sem.at[0])
        if e == 1:
            own_block(0, 512)
        for t, start in enumerate(starts):
            bytes_of(mixed.at[0, :, pl.ds(64, 128), pl.ds(start, size)], swap_sem.at[first + t])
            normalize(start, size)
            across_block(start, size)

    for start in range(512, 2048, 512):
        own_block(start, 512)

    bytes_of(leaving, out_sem)
    bytes_of(leaving, send_sem.at[9])
    bytes_of(mixed.at[0], send_sem.at[8])
    for step in range(3):
        bytes_of(home.at[step, 0, pl.ds(0, NS - 1)], send_sem.at[6])
        bytes_of(home.at[step, 0], send_sem.at[6])
    for c in range(few):
        bytes_of(got.at[c, pl.ds(0, NS - 1)], send_sem.at[1])
    bytes_of(tables.at[0, 0, pl.ds(0, NZ - 1)], send_sem.at[0])
    bytes_of(tables.at[0, pl.ds(0, NXY - 1)], send_sem.at[4])
    bytes_of(tables.at[pl.ds(0, NC - 1)], send_sem.at[5])
    bytes_of(half.at[0], send_sem.at[2])
    bytes_of(own_gate.at[0], send_sem.at[3])


def local(
    stream,
    in_weight,
    in_bias,
    out_weight,
    out_bias,
    first_mix,
    twist_in,
    second_mix,
    kernel,
    third_mix,
    twist_out,
    fourth_mix,
    norm_gain,
    gate_weight,
    up_weight,
    down_weight,
):
    _, width, tokens = stream.shape
    few = width // NS
    fast = pl.BlockSpec(memory_space=pltpu.VMEM)
    slow = pl.BlockSpec(memory_space=pl.ANY)
    wide, half = jnp.float32, BF
    dma = pltpu.SemaphoreType.DMA
    out = pl.pallas_call(
        layer_kernel,
        out_shape=pltpu.VMEM((width, tokens), BF),
        in_specs=[fast] * 7 + [slow] * 9,
        out_specs=fast,
        scratch_shapes=[
            pltpu.VMEM((width, tokens), half),
            pltpu.VMEM(kernel.shape, half),
            pltpu.VMEM((4, 512, 512), half),
            pltpu.VMEM(gate_weight.shape, half),
            pltpu.VMEM(up_weight.shape, half),
            pltpu.VMEM(down_weight.shape, half),
            pltpu.VMEM((4, width, 128), wide),
            pltpu.VMEM((4 * width, 128), wide),
            pltpu.VMEM((16, 512), half),
            pltpu.VMEM((4, 512, 128), wide),
            pltpu.VMEM((few, NS, 16, 512), half),
            pltpu.VMEM((few, NS, 16, 512), half),
            pltpu.VMEM((NC, NXY, NZ, 16, 128), half),
            pltpu.VMEM((512, 512), wide),
            pltpu.VMEM((512, 512), wide),
            pltpu.VMEM((512, 512), wide),
            pltpu.VMEM((3, 2, NS, 16, 128), half),
            pltpu.VMEM((3, 2, NS, 16, 128), half),
            pltpu.VMEM((3, 2, NS * 16, 128), wide),
            pltpu.VMEM((2, width, tokens // 2), half),
            pltpu.VMEM((2, 2, width, 128), wide),
            pltpu.VMEM((2, 2, width, tokens // 2), half),
            pltpu.VMEM((4 * width, width), half),
            pltpu.VMEM((NC, 4 * width, width), half),
            pltpu.VMEM((4 * width, tokens // 2), half),
            pltpu.VMEM((4 * width, 512), half),
            pltpu.VMEM((width, tokens // 2), half),
            dma((9,)),
            dma((10,)),
            dma((few,)),
            dma((3,)),
            dma((3, 2)),
            dma((2,)),
            dma((7,)),
            dma,
            pltpu.SemaphoreType.REGULAR,
            pltpu.SemaphoreType.REGULAR,
        ],
        compiler_params=pltpu.CompilerParams(
            collective_id=0, has_side_effects=True, vmem_limit_bytes=58 * 2**20
        ),
    )(
        in_weight.reshape(1, width),
        in_bias.reshape(1, width),
        out_weight.reshape(1, width),
        out_bias.reshape(1, width),
        norm_gain,
        twist_in.T,
        twist_out.T,
        stream[0],
        kernel,
        first_mix,
        second_mix,
        third_mix,
        fourth_mix,
        gate_weight,
        up_weight,
        down_weight,
    )
    return out[None]


def solution(mesh):
    in_specs = (
        P(None, "ch", "seq"),
        P("ch"),
        P("ch"),
        P("ch"),
        P("ch"),
        P(),
        P(None, "seq"),
        P(),
        P("ch", "seq", None),
        P(),
        P(None, "seq"),
        P(),
        P(),
        P(),
        P(),
        P(),
    )
    out_specs = P(None, "ch", "seq")
    return jax.shard_map(local, mesh=mesh, in_specs=in_specs, out_specs=out_specs, check_vma=False)
```

```python
import jax
import jax.numpy as jnp
from jax import lax
from jax.experimental import pallas as pl
from jax.experimental.pallas import tpu as pltpu
from jax.sharding import PartitionSpec as P

epsilon = 1e-05
MESH = pl.DeviceIdType.MESH
NZ, NX, NY = 8, 4, 2
NXY = NX * NY
NS = NZ * NXY
NC = 4
BF = jnp.bfloat16


def to_wide(array_in):
    return array_in.astype(jnp.float32)


def each_peer(me, core, act):
    z, x, y = lax.div(me, NXY), lax.rem(lax.div(me, NY), NX), lax.rem(me, NY)
    layers = [lax.rem(z + (3 + 2 * core) * low, NZ) * NXY for low in range(NZ)]

    def peer(high, low):
        new_x = lax.rem(x + (high + low) * (1 + 2 * core), NX)
        new_y = lax.rem(y + lax.div(high, NX) + low // NX, NY)
        return layers[low] + new_x * NY + new_y

    for low in range(1, NZ):
        act(peer(jnp.int32(0), low))

    def row(high, carry):
        for low in range(NZ):
            act(peer(high, low))
        return carry

    lax.fori_loop(1, NXY, row, 0)


ROWS = {}
for _step, _parts in enumerate(
    (
        ((0, 0, 10), (1, 0, 6)),
        ((1, 6, 10), (2, 0, 10), (0, 10, 12)),
        ((0, 12, 16), (1, 10, 16), (2, 10, 16)),
    )
):
    _spot = 0
    for _c, _low, _high in _parts:
        for _row in range(_low, _high):
            ROWS[_c, _row] = (_step, _spot)
            _spot += 1


def gate_by(value, score):
    value = 0.5 * value
    return value + value * jnp.tanh(0.5 * score)


def turned_dot(left, right):
    return lax.dot_general(left, right, (((1,), (1,)), ((), ())), preferred_element_type=jnp.float32)


def dot(left, right):
    return jnp.dot(left, right, preferred_element_type=jnp.float32)


def layer_kernel(
    slope_in,
    shift_in,
    slope_out,
    shift_out,
    gain_ref,
    twist_in_ref,
    twist_out_ref,
    stream_any,
    kernel_any,
    first_any,
    second_any,
    third_any,
    fourth_any,
    gate_any,
    up_any,
    down_any,
    out_ref,
    stream_ref,
    kernel_ref,
    mixes,
    gate_ref,
    up_ref,
    down_ref,
    param_ref,
    gains,
    twist_ref,
    gated,
    send,
    got,
    tables,
    table_in,
    table_out,
    held,
    wide_back,
    back,
    home,
    wide_home,
    half,
    own_gate,
    mixed,
    turned,
    chosen,
    normed,
    hidden,
    leaving,
    load_sem,
    send_sem,
    got_sem,
    twist_sem,
    home_sem,
    half_sem,
    swap_sem,
    out_sem,
    plane_sem,
    side_sem,
):
    me = lax.axis_index("seq")
    ch = lax.axis_index("ch")
    core = lax.rem(ch, 2)
    side = lax.div(ch, 2)
    across = (1 - side) * 2 + core
    partner = side * 2 + 1 - core
    my_z, my_xy = lax.div(me, NXY), lax.rem(me, NXY)
    few = got.shape[0]

    loads = [
        pltpu.make_async_copy(source, target, load_sem.at[i])
        for i, (source, target) in enumerate(
            (
                (stream_any, stream_ref),
                (kernel_any, kernel_ref),
                (first_any, mixes.at[0]),
                (second_any, mixes.at[1]),
                (third_any, mixes.at[2]),
                (fourth_any, mixes.at[3]),
                (gate_any, gate_ref),
                (up_any, up_ref),
                (down_any, down_ref),
            )
        )
    ]
    for load in loads:
        load.start()

    barrier = pltpu.get_barrier_semaphore()

    columns = [lax.rem(my_z + 3 * q, NZ) * NXY + my_xy for q in range(1, NZ)]
    planes = [my_z * NXY + lax.rem(my_xy + q, NXY) for q in range(1, NXY)]
    for peer in columns + planes:
        pl.semaphore_signal(barrier, 1, device_id={"seq": peer}, device_id_type=MESH)
    for q in range(1, NC):
        pl.semaphore_signal(barrier, 1, device_id={"ch": lax.rem(ch + q, NC)}, device_id_type=MESH)

    def spread(row):
        return jnp.broadcast_to(row, (128, row.shape[1])).T

    for i, row in enumerate((slope_in, shift_in, slope_out, shift_out)):
        param_ref[i] = spread(row[...])
    twist_ref[...] = jnp.concatenate(
        [to_wide(twist_in_ref[...]), to_wide(twist_out_ref[...])], axis=0
    ).astype(BF)

    def pack(c):
        rows = slice(64 * c, 64 * c + 64)
        slope, shift = param_ref[0, rows, :], param_ref[1, rows, :]

        def one(i, carry):
            for q in range(4):
                lanes = pl.ds(pl.multiple_of(i * 512 + q * 128, 128), 128)
                value = to_wide(stream_ref[rows, lanes])
                value = gate_by(value, value * slope + shift)
                gated[q, pl.ds(i, 64, stride=8), :] = value
            return carry

        lax.fori_loop(0, 8, one, 0)
        for q in range(4):
            lanes = slice(128 * q, 128 * q + 128)
            top = gated[q].reshape(64, 8, 128)
            low = to_wide(kernel_ref[rows, :, lanes])
            send[c, :, :, lanes] = jnp.concatenate([top, low], axis=1).astype(BF)

    def send_lines(c):
        def one(peer):
            pltpu.make_async_remote_copy(
                src_ref=send.at[c, peer],
                dst_ref=got.at[c, me],
                send_sem=send_sem.at[1],
                recv_sem=got_sem.at[c],
                device_id={"seq": peer},
                device_id_type=MESH,
            ).start()

        each_peer(me, core, one)
        got[c, me] = send[c, me]

    def bytes_of(ref, sem):
        pltpu.make_async_copy(ref, ref, sem).wait()

    loads[0].wait()
    loads[1].wait()
    pack(0)
    pl.semaphore_wait(barrier, NZ - 1 + NXY - 1 + NC - 1)
    for peer in planes:
        pl.semaphore_signal(plane_sem, 1, device_id={"seq": peer}, device_id_type=MESH)

    lanes = pl.ds(pl.multiple_of(ch * 128, 128), 128)
    for peer in columns:
        pltpu.make_async_remote_copy(
            src_ref=twist_ref.at[:, lanes],
            dst_ref=tables.at[ch, my_xy, my_z],
            send_sem=send_sem.at[0],
            recv_sem=twist_sem.at[0],
            device_id={"seq": peer},
            device_id_type=MESH,
        ).start()
    tables[ch, my_xy, my_z] = twist_ref[:, lanes]
    pl.semaphore_wait(plane_sem, NXY - 1)
    pl.semaphore_signal(side_sem, 1, device_id={"ch": across}, device_id_type=MESH)
    send_lines(0)
    pack(1)
    send_lines(1)
    bytes_of(tables.at[0, 0, pl.ds(0, NZ - 1)], twist_sem.at[0])
    for peer in planes:
        pltpu.make_async_remote_copy(
            src_ref=tables.at[ch, my_xy],
            dst_ref=tables.at[ch, my_xy],
            send_sem=send_sem.at[4],
            recv_sem=twist_sem.at[1],
            device_id={"seq": peer},
            device_id_type=MESH,
        ).start()
    pack(2)
    send_lines(2)
    bytes_of(tables.at[0, pl.ds(0, NXY - 1)], twist_sem.at[1])
    for q in range(1, NC):
        pltpu.make_async_remote_copy(
            src_ref=tables.at[ch],
            dst_ref=tables.at[ch],
            send_sem=send_sem.at[5],
            recv_sem=twist_sem.at[2],
            device_id={"ch": lax.rem(ch + q, NC)},
            device_id_type=MESH,
        ).start()
    for i in range(8):
        for e in range(2):
            lanes = pl.ds(pl.multiple_of(i * 512 + 256 * (1 - side) + 128 * e, 128), 128)
            pltpu.make_async_remote_copy(
                src_ref=stream_ref.at[:, lanes],
                dst_ref=half.at[side, :, pl.ds(e * 1024 + i * 128, 128)],
                send_sem=send_sem.at[2],
                recv_sem=half_sem.at[0],
                device_id={"ch": across},
                device_id_type=MESH,
            ).start()
    pltpu.make_async_remote_copy(
        src_ref=param_ref.at[pl.ds(2, 2)],
        dst_ref=own_gate.at[side],
        send_sem=send_sem.at[3],
        recv_sem=half_sem.at[1],
        device_id={"ch": across},
        device_id_type=MESH,
    ).start()

    for i in range(8):
        for e in range(2):
            lanes = pl.ds(pl.multiple_of(i * 512 + 256 * side + 128 * e, 128), 128)
            half[side, :, e * 1024 + i * 128 : e * 1024 + i * 128 + 128] = stream_ref[:, lanes]
    own_gate[side] = param_ref[2:4]
    gains[...] = spread(to_wide(gain_ref[...]).reshape(1, 768))

    for load in loads[2:]:
        load.wait()

    def choose(n, carry):
        for w, source in enumerate((gate_ref, up_ref)):
            turned[...] = to_wide(source[n]).T.astype(BF)
            for j, k in enumerate((ch, across)):
                chosen[n, (2 * j + w) * 192 : (2 * j + w + 1) * 192, :] = turned[
                    pl.ds(pl.multiple_of(k * 192, 192), 192), :
                ]
        return carry

    lax.fori_loop(0, NC, choose, 0)

    bytes_of(tables.at[pl.ds(0, NC - 1)], twist_sem.at[2])
    for q in range(NC):
        rows = slice(q * 128, (q + 1) * 128)
        part = to_wide(tables[q])
        part = jnp.concatenate([part[:, z] for z in range(NZ)], axis=0)
        part = part.reshape(NS, 2, 8, 128)
        table_in[rows, :] = part[:, 0].reshape(NS * 8, 128).T
        table_out[rows, :] = part[:, 1].reshape(NS * 8, 128).T

    def arrive(c):
        bytes_of(got.at[c, pl.ds(0, NS - 1)], got_sem.at[c])

    def mix(c):
        block = to_wide(got[c]).reshape(NS, 2, 8, 512)
        lines = block[:, 0].reshape(512, 512).astype(BF)
        value = dot(mixes[0], lines)
        value = (value * table_in[...]).astype(BF)
        value = turned_dot(value, mixes[1])
        block = to_wide(got[c]).reshape(NS, 2, 8, 512)
        value = (value * block[:, 1].reshape(512, 512)).astype(BF)
        value = turned_dot(value, mixes[2])
        value = (to_wide(value.astype(BF)) * table_out[...]).astype(BF)
        return dot(mixes[3], value)

    def spread_rows(c):
        value = mix(c)
        for q in range(4):
            held[q] = value[:, 128 * q : 128 * q + 128]
        for h in range(2):
            for row in range(16):
                step, spot = ROWS[c, row]
                wide_back[step, h, pl.ds(spot, NS, stride=16), :] = held[
                    2 * h + row // 8, pl.ds(row % 8, NS, stride=8), :
                ]

    def finish(step):
        for h in range(2):
            back[step, h] = wide_back[step, h].reshape(NS, 16, 128).astype(BF)

    def send_back(step, same=True, far=True):
        def one(peer, near):
            to_side, to_ch = (side, ch) if near else (1 - side, across)
            pltpu.make_async_remote_copy(
                src_ref=back.at[step, to_side, peer],
                dst_ref=home.at[step, side, me],
                send_sem=send_sem.at[6],
                recv_sem=home_sem.at[step, 0 if near else 1],
                device_id={"seq": peer, "ch": to_ch},
                device_id_type=MESH,
            ).start()

        def both(peer):
            if same:
                one(peer, True)
            if far:
                one(peer, False)

        each_peer(me, core, both)
        if far:
            one(me, False)
        if same:
            home[step, side, me] = back[step, side, me]

    def widen(step):
        bytes_of(home.at[step, 0, pl.ds(0, NS - 1)], home_sem.at[step, 0])
        bytes_of(home.at[step, 0], home_sem.at[step, 1])
        for y in range(2):
            wide_home[step, y] = to_wide(home[step, y]).reshape(NS * 16, 128)

    def gate_out(c, token_row):
        step, spot = ROWS[c, token_row]
        rows = slice(64 * c, 64 * c + 64)
        lanes = slice(token_row * 128, token_row * 128 + 128)

        def one(y, carry):
            slope, shift = own_gate[y, 0, rows, :], own_gate[y, 1, rows, :]
            value = to_wide(half[y, rows, lanes])
            came = wide_home[step, y, pl.ds(spot, 64, stride=16), :]
            value = value + gate_by(came, value * slope + shift)
            mixed[core, y, rows, lanes] = value.astype(BF)
            return carry

        lax.fori_loop(0, 2, one, 0)

    def gate_step(step, low, high):
        for (c, token_row), (where, _) in ROWS.items():
            if where == step and low <= token_row < high:
                gate_out(c, token_row)

    def swap(tokens, sem):
        part = mixed.at[core, :, :, tokens]
        pltpu.make_async_remote_copy(
            src_ref=part,
            dst_ref=part,
            send_sem=send_sem.at[8],
            recv_sem=sem,
            device_id={"ch": partner},
            device_id_type=MESH,
        ).start()

    arrive(0)
    spread_rows(0)
    arrive(1)
    spread_rows(1)
    finish(0)
    pl.semaphore_wait(side_sem, 1)
    send_back(0, same=False)
    arrive(2)
    send_back(0, far=False)
    spread_rows(2)
    finish(1)
    send_back(1)
    finish(2)
    bytes_of(half.at[0], half_sem.at[0])
    bytes_of(own_gate.at[0], half_sem.at[1])
    widen(0)
    gate_step(0, 0, 16)
    send_back(2)

    def normalize(start, size):
        tokens = slice(start, start + size)
        slot = tokens
        total = jnp.zeros((1, size), jnp.float32)
        for n in range(NC):
            value = to_wide(mixed[n % 2, n // 2, :, tokens])
            total = total + jnp.sum(value * value, axis=0, keepdims=True)
        inverse = lax.rsqrt(total / 768.0 + epsilon)
        for n in range(NC):
            value = to_wide(mixed[n % 2, n // 2, :, tokens])
            gain = gains[192 * n : 192 * n + 192, :]
            gain = jnp.concatenate([gain] * (size // 128), axis=1)
            normed[192 * n : 192 * n + 192, slot] = (value * inverse * gain).astype(BF)

    def block(start, size, j):
        tokens = slice(start, start + size)
        slot = tokens
        for n in range(NC):
            wide = dot(
                chosen[n, 384 * j : 384 * j + 384, :], normed[192 * n : 192 * n + 192, slot]
            )
            gate, up = wide[:192], wide[192:]
            hidden[192 * n : 192 * n + 192, :size] = (gate_by(gate, gate) * up).astype(BF)
        value = dot(down_ref[(ch, across)[j]], hidden[:, :size])
        return (to_wide(mixed[core, (side, 1 - side)[j], :, tokens]) + value).astype(BF)

    def place(token):
        start = 512 * (token % 1024 // 128) + 256 * side + 128 * (token // 1024)
        return pl.ds(pl.multiple_of(start, 128), 128)

    def across_block(start, size):
        leaving[:, start : start + size] = block(start, size, 1)
        for token in range(start, start + size, 128):
            pltpu.make_async_remote_copy(
                src_ref=leaving.at[:, pl.ds(token, 128)],
                dst_ref=out_ref.at[:, place(token)],
                send_sem=send_sem.at[9],
                recv_sem=out_sem,
                device_id={"ch": across},
                device_id_type=MESH,
            ).start()

    def own_block(start, size):
        value = block(start, size, 0)
        for i in range(0, size, 128):
            out_ref[:, place(start + i)] = value[:, i : i + 128]

    chunks = ((0, 512), (512, 512), (1024, 256), (1280, 256), (1536, 256), (1792, 256))
    for e, low, high in ((0, 0, 3), (1, 3, 6)):
        widen(1 + e)
        for t in range(low, high):
            start, size = chunks[t]
            for step in range(e, 2 + e):
                if step > 0:
                    gate_step(step, start // 128, (start + size) // 128)
            swap(pl.ds(start, size), swap_sem.at[t])
        if e == 1:
            own_block(0, 512)
        for t in range(low, high):
            start, size = chunks[t]
            bytes_of(mixed.at[0, :, :, pl.ds(start, size)], swap_sem.at[t])
            normalize(start, size)
            across_block(start, size)

    for start in range(512, 2048, 512):
        own_block(start, 512)

    bytes_of(leaving, out_sem)
    bytes_of(leaving, send_sem.at[9])
    bytes_of(mixed.at[0], send_sem.at[8])
    for step in range(3):
        bytes_of(home.at[step, 0, pl.ds(0, NS - 1)], send_sem.at[6])
        bytes_of(home.at[step, 0], send_sem.at[6])
    for c in range(few):
        bytes_of(got.at[c, pl.ds(0, NS - 1)], send_sem.at[1])
    bytes_of(tables.at[0, 0, pl.ds(0, NZ - 1)], send_sem.at[0])
    bytes_of(tables.at[0, pl.ds(0, NXY - 1)], send_sem.at[4])
    bytes_of(tables.at[pl.ds(0, NC - 1)], send_sem.at[5])
    bytes_of(half.at[0], send_sem.at[2])
    bytes_of(own_gate.at[0], send_sem.at[3])


def local(
    stream,
    in_weight,
    in_bias,
    out_weight,
    out_bias,
    first_mix,
    twist_in,
    second_mix,
    kernel,
    third_mix,
    twist_out,
    fourth_mix,
    norm_gain,
    gate_weight,
    up_weight,
    down_weight,
):
    _, width, tokens = stream.shape
    few = width // NS
    fast = pl.BlockSpec(memory_space=pltpu.VMEM)
    slow = pl.BlockSpec(memory_space=pl.ANY)
    wide, half = jnp.float32, BF
    dma = pltpu.SemaphoreType.DMA
    out = pl.pallas_call(
        layer_kernel,
        out_shape=pltpu.VMEM((width, tokens), BF),
        in_specs=[fast] * 7 + [slow] * 9,
        out_specs=fast,
        scratch_shapes=[
            pltpu.VMEM((width, tokens), half),
            pltpu.VMEM(kernel.shape, half),
            pltpu.VMEM((4, 512, 512), half),
            pltpu.VMEM(gate_weight.shape, half),
            pltpu.VMEM(up_weight.shape, half),
            pltpu.VMEM(down_weight.shape, half),
            pltpu.VMEM((4, width, 128), wide),
            pltpu.VMEM((4 * width, 128), wide),
            pltpu.VMEM((16, 512), half),
            pltpu.VMEM((4, 512, 128), wide),
            pltpu.VMEM((few, NS, 16, 512), half),
            pltpu.VMEM((few, NS, 16, 512), half),
            pltpu.VMEM((NC, NXY, NZ, 16, 128), half),
            pltpu.VMEM((512, 512), wide),
            pltpu.VMEM((512, 512), wide),
            pltpu.VMEM((4, 512, 128), wide),
            pltpu.VMEM((3, 2, NS * 16, 128), wide),
            pltpu.VMEM((3, 2, NS, 16, 128), half),
            pltpu.VMEM((3, 2, NS, 16, 128), half),
            pltpu.VMEM((3, 2, NS * 16, 128), wide),
            pltpu.VMEM((2, width, tokens // 2), half),
            pltpu.VMEM((2, 2, width, 128), wide),
            pltpu.VMEM((2, 2, width, tokens // 2), half),
            pltpu.VMEM((4 * width, width), half),
            pltpu.VMEM((NC, 4 * width, width), half),
            pltpu.VMEM((4 * width, tokens // 2), half),
            pltpu.VMEM((4 * width, 512), half),
            pltpu.VMEM((width, tokens // 2), half),
            dma((9,)),
            dma((10,)),
            dma((few,)),
            dma((3,)),
            dma((3, 2)),
            dma((2,)),
            dma((7,)),
            dma,
            pltpu.SemaphoreType.REGULAR,
            pltpu.SemaphoreType.REGULAR,
        ],
        compiler_params=pltpu.CompilerParams(
            collective_id=0, has_side_effects=True, vmem_limit_bytes=58 * 2**20
        ),
    )(
        in_weight.reshape(1, width),
        in_bias.reshape(1, width),
        out_weight.reshape(1, width),
        out_bias.reshape(1, width),
        norm_gain,
        twist_in.T,
        twist_out.T,
        stream[0],
        kernel,
        first_mix,
        second_mix,
        third_mix,
        fourth_mix,
        gate_weight,
        up_weight,
        down_weight,
    )
    return out[None]


def solution(mesh):
    in_specs = (
        P(None, "ch", "seq"),
        P("ch"),
        P("ch"),
        P("ch"),
        P("ch"),
        P(),
        P(None, "seq"),
        P(),
        P("ch", "seq", None),
        P(),
        P(None, "seq"),
        P(),
        P(),
        P(),
        P(),
        P(),
    )
    out_specs = P(None, "ch", "seq")
    return jax.shard_map(local, mesh=mesh, in_specs=in_specs, out_specs=out_specs, check_vma=False)
```
